32 devices in a mesh: stretch: 2 (over x), wide: 8 (over z, y), sect: 2 (over core).
Axes of the slice: x: 2, y: 2, z: 4, core: 2. Of those that a mesh axis runs over, the one named last changes fastest.
Arguments:
- genotypes: int32 [2048, 32768], P(('wide', 'sect'), 'stretch'), parts along dimension 1, may hold values from 0 to 2, as said below
- covariates: float32 [20, 2048], P(None, ('wide', 'sect')), may hold values from -5 to 5, as said below
- phenotypes: float32 [64, 2048], P(None, ('wide', 'sect')), may hold values from -3000 to 3000
- variant_weight: float32 [32768], P('stretch'), parts along dimension 0, may hold values from 0.1 to 10
- gene_start: int32 [128], P('stretch'), parts along dimension 0, may hold values from 0 to 16256, as said below
Outputs:
- burden_z: float32 [128, 64], P('stretch'), parts along dimension 0
- skat_z: float32 [128, 64], P('stretch'), parts along dimension 0
The draws below stay inside these ranges and needn't reach their ends.
There are 2 independent parts, one for each index of `stretch`. The reference program is written for one: setup_inputs(seed, part) draws one part's arguments, and reference() takes and returns one part's arrays. A program takes and returns all parts, laid end to end along the dimension named above; an argument that names none is the same for every part. Nothing has to cross between parts.
Inputs may be any that keep to these rules, and one draw needn't show every extreme that they name: `genotypes`: dosages 0, 1 or 2. `covariates`: row 0 is all ones. gene_start[0] = 0 and starts rise in multiples of 128; each gene spans 1 to 4 blocks of 128 variants, some gene exactly 4.
All inputs are finite; a program needn't handle non-finite values.
Results may differ from the reference program's by a relative error of at most 0.0047.
Values may be sent and summed in bfloat16 or wider, within the bound.
A program may use at most 320 MiB of HBM per device.

```python
import math
import jax
import jax.numpy as jnp
from jax import lax

TRAITS = 64
COVS = 20
BLK = 128
NBLK = 128
GENES = 64
MOST_BLOCKS = 4
VARIANTS = 16384
SAMPLES = 2048


def gene_layout(key):
    size_key, pick_key = jax.random.split(jax.random.fold_in(key, 101))
    gene_sizes = jnp.ones((GENES,), jnp.int32)
    chosen = jax.random.randint(size_key, (), 0, GENES)
    gene_sizes = gene_sizes.at[chosen].set(MOST_BLOCKS)
    spare = NBLK - GENES - (MOST_BLOCKS - 1)

    def add_block(step, current):
        priority = jax.random.randint(jax.random.fold_in(pick_key, step), (GENES,), 0, 1 << 20)
        priority = jnp.where(current < MOST_BLOCKS, priority, -1)
        target = jnp.argmax(priority).astype(jnp.int32)
        return current.at[target].add(1)
    gene_sizes = lax.fori_loop(0, spare, add_block, gene_sizes)
    return gene_sizes


def draw_gene_start(key, part):
    gene_sizes = gene_layout(key)
    starts = jnp.cumsum(gene_sizes) - gene_sizes
    return (starts * BLK).astype(jnp.int32)


def ancestry(count):
    sample_index = jnp.arange(count, dtype=jnp.int32)
    return (sample_index * 2531 + 17) % 1021 % 16


def allele_draw(own_key, share_key, threshold):
    own_value = jax.random.randint(own_key, (SAMPLES, VARIANTS), 0, 10000)
    shared_value = jax.random.randint(share_key, (SAMPLES, NBLK), 0, 1000)
    shared_full = jnp.repeat(shared_value, BLK, axis=1)
    chosen_value = jnp.where(own_value < 9000, shared_full, own_value - 9000)
    return (chosen_value < threshold).astype(jnp.int32)


def draw_genotypes(key, part):
    key = jax.random.fold_in(key, 5)
    level_key, freq_key, factor_key, first_key, second_key, share_first, share_second = jax.random.split(key, 7)
    level = jax.random.randint(level_key, (VARIANTS,), 0, 5)
    base_freq = jnp.left_shift(jnp.full((VARIANTS,), 20, jnp.int32), level)
    per_mille = base_freq + jax.random.randint(freq_key, (VARIANTS,), 0, base_freq)
    group_factor = jax.random.randint(factor_key, (16, VARIANTS), 2, 11)
    group_table = jnp.minimum(per_mille[None, :] * group_factor // 4, 950)
    threshold = jnp.take(group_table, ancestry(SAMPLES), axis=0)
    first_allele = allele_draw(first_key, share_first, threshold)
    second_allele = allele_draw(second_key, share_second, threshold)
    return first_allele + second_allele


def covariate_matrix(key):
    noise_key, load_key = jax.random.split(jax.random.fold_in(key, 303))
    loading = jnp.clip(jax.random.normal(load_key, (COVS - 1, 16), jnp.float32), -3.0, 3.0) * 0.8
    noise = jnp.clip(jax.random.normal(noise_key, (COVS - 1, SAMPLES), jnp.float32), -5.0, 5.0) * 0.5
    rows = jnp.clip(jnp.take(loading, ancestry(SAMPLES), axis=1) + noise, -5.0, 5.0)
    return jnp.concatenate([jnp.ones((1, SAMPLES), jnp.float32), rows], axis=0)


def draw_covariates(key, part):
    full_cov = covariate_matrix(key)
    return full_cov


def draw_phenotypes(key, part):
    full_cov = covariate_matrix(key)
    key = jax.random.fold_in(key, 11)
    effect_key, sample_key, noise_key, trait_key = jax.random.split(key, 4)
    effect = jnp.clip(jax.random.normal(effect_key, (TRAITS, COVS), jnp.float32), -4.0, 4.0) * 0.3
    explained = jnp.dot(effect, full_cov, precision=lax.Precision.HIGHEST)
    position = jnp.arange(SAMPLES, dtype=jnp.float32) / (SAMPLES - 1)
    sample_scale = (1.0 + 2.0 * position)[None, :] * jnp.exp(jax.random.uniform(sample_key, (1, SAMPLES), jnp.float32, 0.0, math.log(3.0)))
    noise = jnp.clip(jax.random.normal(noise_key, (TRAITS, SAMPLES), jnp.float32), -5.0, 5.0)
    trait_scale = jnp.exp(jax.random.uniform(trait_key, (TRAITS, 1), jnp.float32, 0.0, math.log(10.0)))
    return trait_scale * (explained + noise * sample_scale)


def setup_inputs(seed: int = 0, part: int = 0) -> dict:
    seeds = jax.random.split(jax.random.key(seed), 6)
    part_splits = jax.random.split(jax.random.fold_in(seeds[5], part), 6)
    return {
        "genotypes": draw_genotypes(jax.random.fold_in(jax.random.fold_in(seeds[5], part), 71), part),
        "covariates": draw_covariates(jax.random.fold_in(seeds[5], 71), part),
        "phenotypes": draw_phenotypes(jax.random.fold_in(seeds[5], 71), part),
        "variant_weight": jnp.clip(jnp.exp(jax.random.uniform(part_splits[3], (VARIANTS,), jnp.float32, math.log(0.1), math.log(10.0))), 0.1, 10.0),
        "gene_start": draw_gene_start(jax.random.fold_in(jax.random.fold_in(seeds[5], part), 71), part),
    }


PRECISE = lax.Precision.HIGHEST

def reference(genotypes, covariates, phenotypes, variant_weight, gene_start):
    dosage = genotypes.astype(jnp.float32)
    cov_gram = jnp.dot(covariates, covariates.T, precision=PRECISE)
    cov_geno = jnp.dot(covariates, dosage, precision=PRECISE)
    cov_pheno = jnp.dot(covariates, phenotypes.T, precision=PRECISE)
    factor = jnp.linalg.cholesky(cov_gram)
    coef_geno = jax.scipy.linalg.cho_solve((factor, True), cov_geno)
    coef_pheno = jax.scipy.linalg.cho_solve((factor, True), cov_pheno)
    resid_geno = (dosage - jnp.dot(covariates.T, coef_geno, precision=PRECISE)).astype(jnp.bfloat16)
    resid_pheno = phenotypes - jnp.dot(coef_pheno.T, covariates, precision=PRECISE)
    sigma_sq = lax.optimization_barrier(jnp.sum(resid_pheno * resid_pheno, axis=1)) / (SAMPLES - COVS)
    pheno_low = resid_pheno.astype(jnp.bfloat16)
    scores = jnp.dot(pheno_low.astype(jnp.float32), resid_geno.astype(jnp.float32), preferred_element_type=jnp.float32)
    gene_span = MOST_BLOCKS * BLK
    padded_geno = jnp.concatenate([resid_geno, jnp.zeros((SAMPLES, gene_span), jnp.bfloat16)], axis=1)
    padded_scores = jnp.concatenate([scores, jnp.zeros((TRAITS, gene_span), jnp.float32)], axis=1)
    padded_weight = jnp.concatenate([variant_weight, jnp.zeros((gene_span,), jnp.float32)])
    gene_ends = jnp.concatenate([gene_start[1:], jnp.full((1,), VARIANTS, jnp.int32)])

    def one_gene(index):
        begin = gene_start[index].astype(jnp.int32)
        length = gene_ends[index] - begin
        zero_index = jnp.zeros((), jnp.int32)
        columns = lax.dynamic_slice(padded_geno, (zero_index, begin), (SAMPLES, gene_span))
        gene_scores = lax.dynamic_slice(padded_scores, (zero_index, begin), (TRAITS, gene_span))
        inside = jnp.arange(gene_span, dtype=jnp.int32) < length
        weight = jnp.where(inside, lax.dynamic_slice(padded_weight, (begin,), (gene_span,)), jnp.zeros((gene_span,), jnp.float32))
        gene_gram = jnp.dot(columns.T.astype(jnp.float32), columns.astype(jnp.float32), preferred_element_type=jnp.float32)
        burden_var = jnp.dot(weight, jnp.dot(gene_gram, weight, precision=PRECISE), precision=PRECISE)
        weight_sq = weight * weight
        null_mean = jnp.sum(weight_sq * jnp.diagonal(gene_gram))
        null_var = 2.0 * jnp.dot(weight_sq, jnp.dot(gene_gram * gene_gram, weight_sq, precision=PRECISE), precision=PRECISE)
        burden_sum = jnp.dot(gene_scores, weight, precision=PRECISE)
        skat_sum = jnp.dot(gene_scores * gene_scores, weight_sq, precision=PRECISE)
        burden_row = burden_sum / jnp.sqrt(burden_var * sigma_sq + 1e-06)
        skat_row = (skat_sum / sigma_sq - null_mean) / jnp.sqrt(null_var + 1e-06)
        return (burden_row, skat_row)
    burden_z, skat_z = lax.map(one_gene, jnp.arange(GENES, dtype=jnp.int32))
    return (burden_z, skat_z)
```

```python
import functools

import jax
import jax.numpy as jnp
from jax import lax
from jax.experimental import pallas as pl
from jax.experimental.pallas import tpu as pltpu
from jax.sharding import PartitionSpec as P

BLK = 128
MOST = 4
HALO = MOST - 1
PAD_COV = 24
STAT = 256
F32 = jnp.float32
BF16 = jnp.bfloat16
EXACT = lax.Precision.HIGHEST


def dot(a, b, ca, cb, precision=None):
    return lax.dot_general(
        a, b, (((ca,), (cb,)), ((), ())), precision=precision, preferred_element_type=F32
    )


def kernel(
    n, cov, traits, genes, nb,
    geno, cov_ref, phe_ref, w_ref, bounds_ref,
    burden_ref, skat_ref,
    stage, sendbuf, recv, xloc, xall, cx_send, cx_recv, m_send, m_recv,
    lhs, g_send, g_own, g_recv, z_send, z_own, z_recv, stat_loc, stat_all,
    stage_sem, own_sem, d_send, d_recv, x_send, x_recv, e_send, e_recv, s_send, s_recv,
):
    me = lax.axis_index("wide")
    sect = lax.axis_index("sect")
    lin = me * 2 + sect
    rows = geno.shape[0]
    hb = nb // 2
    width = nb * BLK
    span = (nb + HALO) * BLK
    half = hb * BLK
    half_span = (hb + HALO) * BLK
    dof = rows * n * 2 - cov
    peer = {"sect": 1 - sect}

    def chunk_copy(c):
        cols = pl.ds(pl.multiple_of(c * width, BLK), width)
        return pltpu.make_async_copy(geno.at[:, cols], stage.at[:, cols], stage_sem.at[c])

    def start_chunk(t, carry):
        chunk_copy(lax.rem(me - t + n, n)).start()
        return carry

    lax.fori_loop(0, n, start_chunk, 0)

    xloc[...] = jnp.zeros_like(xloc)
    xloc[0:cov, :] = cov_ref[...]
    xloc[PAD_COV:PAD_COV + traits, :] = phe_ref[...]
    xall[...] = jnp.zeros_like(xall)
    sendbuf[:, n * width:] = jnp.zeros((rows, HALO * BLK), BF16)

    barrier = pltpu.get_barrier_semaphore()

    def greet(q, carry):
        p = lax.rem(lin + q, 2 * n)
        pl.semaphore_signal(
            barrier, inc=1, device_id={"wide": p // 2, "sect": lax.rem(p, 2)},
            device_id_type=pl.DeviceIdType.MESH,
        )
        return carry

    lax.fori_loop(1, 2 * n, greet, 0)
    pl.semaphore_wait(barrier, 2 * n - 1)

    xrows = PAD_COV + traits

    def x_copy(t):
        return pltpu.make_async_remote_copy(
            src_ref=xloc,
            dst_ref=xall.at[0:xrows, pl.ds(pl.multiple_of(me * rows, BLK), rows)],
            send_sem=x_send.at[t], recv_sem=x_recv.at[t],
            device_id={"wide": lax.rem(me - t + n, n)},
            device_id_type=pl.DeviceIdType.MESH,
        )

    def d_copy(t):
        c = lax.rem(me - t + n, n)
        return pltpu.make_async_remote_copy(
            src_ref=sendbuf.at[:, pl.ds(pl.multiple_of(c * width, BLK), span)],
            dst_ref=recv.at[me],
            send_sem=d_send.at[t], recv_sem=d_recv.at[t],
            device_id={"wide": c},
            device_id_type=pl.DeviceIdType.MESH,
        )

    def start_x(t, carry):
        x_copy(t).start()
        return carry

    lax.fori_loop(1, n, start_x, 0)
    xall[0:xrows, pl.ds(pl.multiple_of(me * rows, BLK), rows)] = xloc[...]

    def convert(c):
        chunk_copy(c).wait()
        cols = pl.ds(pl.multiple_of(c * width, BLK), width)
        sendbuf[:, cols] = stage[:, cols].astype(F32).astype(BF16)

    convert(me)

    def send_chunk(t, carry):
        convert(lax.rem(me - t + n, n))
        d_copy(t).start()
        return carry

    lax.fori_loop(1, n, send_chunk, 0)
    own_copy = pltpu.make_async_copy(
        sendbuf.at[:, pl.ds(pl.multiple_of(me * width, BLK), span)], recv.at[me], own_sem
    )
    own_copy.start()

    def wait_x(t, carry):
        x_copy(t).wait()
        return carry

    lax.fori_loop(1, n, wait_x, 0)

    def peer_copy(src, dst, k):
        return pltpu.make_async_remote_copy(
            src_ref=src, dst_ref=dst, send_sem=e_send.at[k], recv_sem=e_recv.at[k],
            device_id=peer, device_id_type=pl.DeviceIdType.MESH,
        )

    call = xall[0:PAD_COV, :]
    cx_send[...] = dot(call, xall[...], 1, 1, EXACT)
    cx_copy = peer_copy(cx_send, cx_recv, 0)
    cx_copy.start()
    cx_copy.wait()
    row = lax.broadcasted_iota(jnp.int32, (PAD_COV, BLK), 0)
    lane = lax.broadcasted_iota(jnp.int32, (PAD_COV, BLK), 1)
    mat = cx_send[...] + cx_recv[...] + jnp.where(lane == row + 96, 1.0, 0.0).astype(F32)
    for j in range(cov):
        scale = 1.0 / jnp.sqrt(mat[j:j + 1, j:j + 1])
        row_j = mat[j:j + 1, :] * scale
        col_j = mat[:, j:j + 1] * scale
        mat = jnp.where(row > j, mat - col_j * row_j, jnp.where(row == j, row_j, mat))
    proj = mat[:, PAD_COV:PAD_COV + traits]
    low_inv = mat[:, 96:96 + PAD_COV]
    cov_unit = dot(low_inv, call, 1, 0, EXACT)
    resid = xall[PAD_COV:PAD_COV + traits, :] - dot(proj, cov_unit, 0, 0, EXACT)
    resid_low = resid.astype(BF16)
    lhs[...] = jnp.zeros_like(lhs)
    lhs[0:traits, :] = resid_low
    hi = cov_unit.astype(BF16)
    rest = cov_unit - hi.astype(F32)
    mid = rest.astype(BF16)
    low = (rest - mid.astype(F32)).astype(BF16)
    lhs[traits:traits + PAD_COV, :] = hi
    lhs[traits + 32:traits + 32 + PAD_COV, :] = mid
    lhs[traits + 64:traits + 64 + PAD_COV, :] = low
    m_send[0:PAD_COV, :] = dot(cov_unit, resid_low.astype(F32), 1, 1, EXACT)
    ones = jnp.ones((8, resid.shape[1]), F32)
    m_send[PAD_COV:PAD_COV + 8, :] = dot(ones, resid * resid, 1, 1, EXACT)
    m_copy = peer_copy(m_send, m_recv, 1)
    m_copy.start()
    m_copy.wait()
    cross = m_send[0:PAD_COV, :] + m_recv[0:PAD_COV, :]
    sigma_sq = (m_send[PAD_COV:PAD_COV + 1, :] + m_recv[PAD_COV:PAD_COV + 1, :]) / dof

    own_copy.wait()

    def wait_d(t, carry):
        d_copy(t).wait()
        return carry

    lax.fori_loop(1, n, wait_d, 0)

    def partial(which, gram, z_out):
        base = which * half

        def one_block(j, carry):
            at = base + j * BLK
            left = recv[:, :, pl.ds(pl.multiple_of(at, BLK), BLK)].reshape(n * rows, BLK)
            right = recv[:, :, pl.ds(pl.multiple_of(at, BLK), MOST * BLK)]
            gram[j] = dot(left, right.reshape(n * rows, MOST * BLK), 0, 0)
            return carry

        lax.fori_loop(0, hb, one_block, 0)

    def partial_z(which, z_out):
        base = pl.multiple_of(which * half, BLK)
        data = recv[:, :, pl.ds(base, half_span)].reshape(n * rows, half_span)
        full = dot(lhs[...], data, 1, 0)
        z_out[0:traits, :] = full[0:traits]
        z_out[traits:traits + 32, :] = (
            full[traits:traits + 32] + full[traits + 32:traits + 64] + full[traits + 64:traits + 96]
        )

    partial(1 - sect, g_send, z_send)
    g_copy = peer_copy(g_send, g_recv, 2)
    g_copy.start()
    partial_z(1 - sect, z_send)
    z_copy = peer_copy(z_send, z_recv, 3)
    z_copy.start()
    partial(sect, g_own, z_own)
    partial_z(sect, z_own)
    z_copy.wait()
    g_copy.wait()

    zs = z_own[...] + z_recv[...]
    z = zs[traits:traits + PAD_COV]
    scores = zs[0:traits, 0:half] - dot(cross, z[:, 0:half], 0, 0, EXACT)

    weight = w_ref[...]
    weight_t = jnp.transpose(
        jnp.concatenate([weight, jnp.zeros((BLK - weight.shape[0], BLK), F32)], axis=0)
    )
    r8 = lax.broadcasted_iota(jnp.int32, (8, BLK), 0)
    l8 = lax.broadcasted_iota(jnp.int32, (8, BLK), 1)
    spread = jnp.concatenate(
        [jnp.where(r8 == j, weight[0:8], 0.0) for j in range(hb)], axis=1
    )
    stat_loc[:, 0:traits] = dot(spread, scores, 1, 1, EXACT)
    stat_loc[:, traits:2 * traits] = dot(spread * spread, scores * scores, 1, 1, EXACT)
    eye = jnp.where(
        lax.broadcasted_iota(jnp.int32, (BLK, BLK), 0)
        == lax.broadcasted_iota(jnp.int32, (BLK, BLK), 1), 1.0, 0.0,
    ).astype(F32)
    lin_rows, sq_rows, diag_rows = [], [], []
    for j in range(hb):
        g = g_own[j] + g_recv[j]
        g = g - dot(z[:, j * BLK:(j + 1) * BLK], z[:, j * BLK:(j + MOST) * BLK], 0, 0, EXACT)
        w_col = weight_t[:, j:j + 1]
        lin_rows.append(jnp.sum(g * w_col, axis=0, keepdims=True))
        sq_rows.append(jnp.sum(g * g * (w_col * w_col), axis=0, keepdims=True))
        diag_rows.append(jnp.sum(g[:, 0:BLK] * eye, axis=0, keepdims=True))
    if hb < 8:
        zero = jnp.zeros((8 - hb, MOST * BLK), F32)
        lin_rows.append(zero)
        sq_rows.append(zero)
        diag_rows.append(zero[:, 0:BLK])
    lin_all = jnp.concatenate(lin_rows, axis=0)
    sq_all = jnp.concatenate(sq_rows, axis=0)
    diag_all = jnp.concatenate(diag_rows, axis=0)
    packed = jnp.zeros((8, BLK), F32)
    for k in range(MOST):
        w_k = weight[k:k + 8]
        twice = 1.0 if k == 0 else 2.0
        first = jnp.sum(lin_all[:, k * BLK:(k + 1) * BLK] * w_k, axis=1, keepdims=True)
        second = jnp.sum(sq_all[:, k * BLK:(k + 1) * BLK] * (w_k * w_k), axis=1, keepdims=True)
        packed = jnp.where(l8 == 2 * k, twice * first, packed)
        packed = jnp.where(l8 == 2 * k + 1, twice * second, packed)
    mean_part = jnp.sum(diag_all * weight[0:8] * weight[0:8], axis=1, keepdims=True)
    packed = jnp.where(l8 == 2 * MOST, mean_part, packed)
    stat_loc[:, 2 * traits:] = packed

    def s_copy(q):
        p = lax.rem(lin + q, 2 * n)
        return pltpu.make_async_remote_copy(
            src_ref=stat_loc,
            dst_ref=stat_all.at[pl.ds(pl.multiple_of(lin * 8, 8), 8)],
            send_sem=s_send.at[q], recv_sem=s_recv.at[q],
            device_id={"wide": p // 2, "sect": lax.rem(p, 2)},
            device_id_type=pl.DeviceIdType.MESH,
        )

    def start_s(q, carry):
        s_copy(q).start()
        return carry

    def wait_s(q, carry):
        s_copy(q).wait()
        return carry

    lax.fori_loop(1, 2 * n, start_s, 0)
    stat_all[pl.ds(pl.multiple_of(lin * 8, 8), 8), :] = stat_loc[...]
    lax.fori_loop(1, 2 * n, wait_s, 0)

    slots = 2 * n * 8
    slot = lax.broadcasted_iota(jnp.int32, (genes, slots), 1)
    within = lax.rem(slot, 8)
    first_variant = ((slot // 8) * hb + within) * BLK
    begin = bounds_ref[:, 0:1]
    end = bounds_ref[:, 1:2]
    member = (within < hb) & (first_variant >= begin) & (first_variant < end)
    sums = dot(jnp.where(member, 1.0, 0.0).astype(F32), stat_all[...], 1, 0, EXACT)
    burden_var = sums[:, 2 * traits:2 * traits + 1]
    null_var = sums[:, 2 * traits + 1:2 * traits + 2]
    null_mean = sums[:, 2 * traits + 2 * MOST:2 * traits + 2 * MOST + 1]
    for k in range(1, MOST):
        inside = member & (first_variant + k * BLK < end)
        pair = dot(
            jnp.where(inside, 1.0, 0.0).astype(F32), stat_all[:, 2 * traits:], 1, 0, EXACT
        )
        burden_var = burden_var + pair[:, 2 * k:2 * k + 1]
        null_var = null_var + pair[:, 2 * k + 1:2 * k + 2]
    null_var = 2.0 * null_var
    burden_ref[...] = sums[:, 0:traits] / jnp.sqrt(burden_var * sigma_sq + 1e-06)
    skat_ref[...] = (sums[:, traits:2 * traits] / sigma_sq - null_mean) / jnp.sqrt(null_var + 1e-06)


def body(genotypes, covariates, phenotypes, variant_weight, gene_start):
    rows, variants = genotypes.shape
    cov = covariates.shape[0]
    traits = phenotypes.shape[0]
    genes = gene_start.shape[0]
    n = lax.axis_size("wide")
    nb = variants // BLK // n
    hb = nb // 2
    span = (nb + HALO) * BLK
    half_span = (hb + HALO) * BLK
    lin = lax.axis_index("wide") * 2 + lax.axis_index("sect")
    padded = jnp.concatenate(
        [variant_weight.reshape(-1, BLK), jnp.zeros((16, BLK), F32)], axis=0
    )
    weight = lax.dynamic_slice(padded, (lin * hb, 0), (16, BLK))
    ends = jnp.concatenate([gene_start[1:], jnp.full((1,), variants, jnp.int32)])
    bounds = jnp.stack([gene_start, ends], axis=1)
    vmem = pl.BlockSpec(memory_space=pltpu.VMEM)
    samples = n * rows
    dma = pltpu.SemaphoreType.DMA
    return pl.pallas_call(
        functools.partial(kernel, n, cov, traits, genes, nb),
        out_shape=(
            jax.ShapeDtypeStruct((genes, traits), F32),
            jax.ShapeDtypeStruct((genes, traits), F32),
        ),
        in_specs=[pl.BlockSpec(memory_space=pl.ANY), vmem, vmem, vmem, vmem],
        out_specs=(vmem, vmem),
        scratch_shapes=[
            pltpu.VMEM((rows, variants), jnp.int32),
            pltpu.VMEM((rows, variants + HALO * BLK), BF16),
            pltpu.VMEM((n, rows, span), BF16),
            pltpu.VMEM((PAD_COV + traits, rows), F32),
            pltpu.VMEM((BLK, samples), F32),
            pltpu.VMEM((PAD_COV, BLK), F32),
            pltpu.VMEM((PAD_COV, BLK), F32),
            pltpu.VMEM((PAD_COV + 8, traits), F32),
            pltpu.VMEM((PAD_COV + 8, traits), F32),
            pltpu.VMEM((traits + 96, samples), BF16),
            pltpu.VMEM((hb, BLK, MOST * BLK), F32),
            pltpu.VMEM((hb, BLK, MOST * BLK), F32),
            pltpu.VMEM((hb, BLK, MOST * BLK), F32),
            pltpu.VMEM((traits + 32, half_span), F32),
            pltpu.VMEM((traits + 32, half_span), F32),
            pltpu.VMEM((traits + 32, half_span), F32),
            pltpu.VMEM((8, STAT), F32),
            pltpu.VMEM((2 * n * 8, STAT), F32),
            dma((n,)), dma, dma((n,)), dma((n,)), dma((n,)), dma((n,)),
            dma((4,)), dma((4,)), dma((2 * n,)), dma((2 * n,)),
        ],
        compiler_params=pltpu.CompilerParams(
            collective_id=0, has_side_effects=True, vmem_limit_bytes=56 * 1024 * 1024
        ),
        cost_estimate=pl.CostEstimate(
            flops=4 * samples * nb * BLK * MOST * BLK,
            bytes_accessed=rows * variants * 4, transcendentals=0,
        ),
    )(genotypes, covariates, phenotypes, weight, bounds)


def solution(mesh):
    placed = (
        P(("wide", "sect"), "stretch"),
        P(None, ("wide", "sect")),
        P(None, ("wide", "sect")),
        P("stretch"),
        P("stretch"),
    )
    return jax.shard_map(
        body,
        mesh=mesh,
        in_specs=placed,
        out_specs=(P("stretch", None), P("stretch", None)),
        check_vma=False,
    )
```

```python
import functools

import jax
import jax.numpy as jnp
from jax import lax
from jax.experimental import pallas as pl
from jax.experimental.pallas import tpu as pltpu
from jax.sharding import PartitionSpec as P

BLK = 128
MOST = 4
HALO = MOST - 1
PAD_COV = 24
STAT = 256
F32 = jnp.float32
BF16 = jnp.bfloat16
EXACT = lax.Precision.HIGHEST


def dot(a, b, ca, cb, precision=None):
    return lax.dot_general(
        a, b, (((ca,), (cb,)), ((), ())), precision=precision, preferred_element_type=F32
    )


def kernel(
    n, cov, traits, genes, nb,
    geno, cov_ref, phe_ref, w_ref, bounds_ref,
    burden_ref, skat_ref,
    stage, sendbuf, recv, xloc, xall, cx_send, cx_recv, m_send, m_recv,
    lhs, g_send, g_own, g_recv, s_send, s_own, sc_recv, z_send, z_own, z_recv, stat_loc, stat_all,
    stage_sem, own_sem, d_send, d_recv, x_send, x_recv, e_send, e_recv, t_send, t_recv, gs_sem, gr_sem,
):
    wide = lax.axis_index("wide")
    member = n // 2
    side = wide // member
    me = lax.rem(wide, member) * 2 + lax.axis_index("sect")
    lin = me * 2 + side

    def place(group, at_side):
        return {"wide": at_side * member + group // 2, "sect": lax.rem(group, 2)}

    rows = geno.shape[0]
    hb = nb // 2
    width = nb * BLK
    span = (nb + HALO) * BLK
    half = hb * BLK
    half_span = (hb + HALO) * BLK
    dof = rows * n * 2 - cov
    peer = {"wide": (1 - side) * member + lax.rem(wide, member)}

    def chunk_copy(c):
        cols = pl.ds(pl.multiple_of(c * width, BLK), width)
        return pltpu.make_async_copy(geno.at[:, cols], stage.at[:, cols], stage_sem.at[c])

    def start_chunk(t, carry):
        chunk_copy(lax.rem(me - t + n, n)).start()
        return carry

    lax.fori_loop(0, n, start_chunk, 0)

    xloc[...] = jnp.zeros_like(xloc)
    xloc[0:cov, :] = cov_ref[...]
    xloc[PAD_COV:PAD_COV + traits, :] = phe_ref[...]
    xall[...] = jnp.zeros_like(xall)
    sendbuf[:, n * width:] = jnp.zeros((rows, HALO * BLK), BF16)

    barrier = pltpu.get_barrier_semaphore()

    def greet(q, carry):
        p = lax.rem(lin + q, 2 * n)
        pl.semaphore_signal(
            barrier, inc=1, device_id=place(p // 2, lax.rem(p, 2)),
            device_id_type=pl.DeviceIdType.MESH,
        )
        return carry

    lax.fori_loop(1, 2 * n, greet, 0)
    pl.semaphore_wait(barrier, 2 * n - 1)

    xrows = PAD_COV + traits

    def x_copy(t):
        return pltpu.make_async_remote_copy(
            src_ref=xloc,
            dst_ref=xall.at[0:xrows, pl.ds(pl.multiple_of(me * rows, BLK), rows)],
            send_sem=x_send.at[t], recv_sem=x_recv.at[t],
            device_id=place(lax.rem(me - t + n, n), side),
            device_id_type=pl.DeviceIdType.MESH,
        )

    def d_part(t, part, offset, size):
        c = lax.rem(me - t + n, n)
        return pltpu.make_async_remote_copy(
            src_ref=sendbuf.at[:, pl.ds(pl.multiple_of(c * width + offset, BLK), size)],
            dst_ref=recv.at[me, :, pl.ds(pl.multiple_of(offset, BLK), size)],
            send_sem=d_send.at[part, t], recv_sem=d_recv.at[part, t],
            device_id=place(c, side),
            device_id_type=pl.DeviceIdType.MESH,
        )

    def d_first(t):
        return d_part(t, 0, (1 - side) * half, half_span)

    def d_second(t):
        return d_part(t, 1, side * half_span, half)

    def start_x(t, carry):
        x_copy(t).start()
        return carry

    lax.fori_loop(1, n, start_x, 0)
    xall[0:xrows, pl.ds(pl.multiple_of(me * rows, BLK), rows)] = xloc[...]

    def convert(c):
        chunk_copy(c).wait()
        cols = pl.ds(pl.multiple_of(c * width, BLK), width)
        sendbuf[:, cols] = stage[:, cols].astype(F32).astype(BF16)

    convert(me)

    def send_chunk(t, carry):
        convert(lax.rem(me - t + n, n))
        d_first(t).start()
        return carry

    def send_second(t, carry):
        d_second(t).start()
        return carry

    lax.fori_loop(1, n, send_chunk, 0)
    lax.fori_loop(1, n, send_second, 0)
    own_copy = pltpu.make_async_copy(
        sendbuf.at[:, pl.ds(pl.multiple_of(me * width, BLK), span)], recv.at[me], own_sem
    )
    own_copy.start()

    def wait_x(t, carry):
        x_copy(t).wait()
        return carry

    lax.fori_loop(1, n, wait_x, 0)

    def peer_copy(src, dst, k):
        return pltpu.make_async_remote_copy(
            src_ref=src, dst_ref=dst, send_sem=e_send.at[k], recv_sem=e_recv.at[k],
            device_id=peer, device_id_type=pl.DeviceIdType.MESH,
        )

    call = xall[0:PAD_COV, :]
    cx_send[...] = dot(call, xall[...], 1, 1, EXACT)
    cx_copy = peer_copy(cx_send, cx_recv, 0)
    cx_copy.start()
    cx_copy.wait()
    row = lax.broadcasted_iota(jnp.int32, (PAD_COV, BLK), 0)
    lane = lax.broadcasted_iota(jnp.int32, (PAD_COV, BLK), 1)
    mat = cx_send[...] + cx_recv[...] + jnp.where(lane == row + 96, 1.0, 0.0).astype(F32)
    for j in range(cov):
        scale = 1.0 / jnp.sqrt(mat[j:j + 1, j:j + 1])
        row_j = mat[j:j + 1, :] * scale
        col_j = mat[:, j:j + 1] * scale
        mat = jnp.where(row > j, mat - col_j * row_j, jnp.where(row == j, row_j, mat))
    proj = mat[:, PAD_COV:PAD_COV + traits]
    low_inv = mat[:, 96:96 + PAD_COV]
    cov_unit = dot(low_inv, call, 1, 0, EXACT)
    resid = xall[PAD_COV:PAD_COV + traits, :] - dot(proj, cov_unit, 0, 0, EXACT)
    resid_low = resid.astype(BF16)
    lhs[...] = jnp.zeros_like(lhs)
    lhs[0:traits, :] = resid_low
    hi = cov_unit.astype(BF16)
    rest = cov_unit - hi.astype(F32)
    mid = rest.astype(BF16)
    low = (rest - mid.astype(F32)).astype(BF16)
    lhs[traits:traits + PAD_COV, :] = hi
    lhs[traits + 32:traits + 32 + PAD_COV, :] = mid
    lhs[traits + 24:traits + 32, :] = jnp.ones((8, lhs.shape[1]), BF16)
    lhs[traits + 64:traits + 64 + PAD_COV, :] = low
    m_send[0:PAD_COV, :] = dot(cov_unit, resid_low.astype(F32), 1, 1, EXACT)
    ones = jnp.ones((8, resid.shape[1]), F32)
    m_send[PAD_COV:PAD_COV + 8, :] = dot(ones, resid * resid, 1, 1, EXACT)
    m_copy = peer_copy(m_send, m_recv, 1)
    m_copy.start()
    m_copy.wait()
    cross = m_send[0:PAD_COV, :] + m_recv[0:PAD_COV, :]
    sigma_sq = (m_send[PAD_COV:PAD_COV + 1, :] + m_recv[PAD_COV:PAD_COV + 1, :]) / dof

    own_copy.wait()

    def wait_first(t, carry):
        d_first(t).wait()
        return carry

    def wait_second(t, carry):
        d_second(t).wait()
        return carry

    def gram(which, j):
        at = pl.multiple_of(which * half + j * BLK, BLK)
        left = recv[:, :, pl.ds(at, BLK)].reshape(n * rows, BLK)
        right = recv[:, :, pl.ds(at, MOST * BLK)].reshape(n * rows, MOST * BLK)
        return dot(left, right, 0, 0)

    def project(which, s_out, z_out):
        base = pl.multiple_of(which * half, BLK)
        data = recv[:, :, pl.ds(base, half_span)].reshape(n * rows, half_span)
        full = dot(lhs[...], data, 1, 0)
        s_out[...] = full[0:traits, 0:half]
        z_out[...] = (
            full[traits:traits + 32] + full[traits + 32:traits + 64] + full[traits + 64:traits + 96]
        )

    shrink = 1.0 / float(n * rows) ** 0.5

    def g_copy(j):
        return pltpu.make_async_remote_copy(
            src_ref=g_send.at[j], dst_ref=g_recv.at[j],
            send_sem=gs_sem.at[j], recv_sem=gr_sem.at[j],
            device_id=peer, device_id_type=pl.DeviceIdType.MESH,
        )

    lax.fori_loop(1, n, wait_first, 0)
    project(1 - side, s_send, z_send)
    z_copy = peer_copy(z_send, z_recv, 2)
    z_copy.start()
    sum_row = lax.broadcasted_iota(jnp.int32, (8, half_span), 0) == 0

    def send_gram(j, carry):
        left = z_send[PAD_COV:32, pl.ds(pl.multiple_of(j * BLK, BLK), BLK)]
        right = z_send[PAD_COV:32, pl.ds(pl.multiple_of(j * BLK, BLK), MOST * BLK)]
        left = jnp.where(sum_row[:, 0:BLK], left * shrink, 0.0)
        right = jnp.where(sum_row[:, 0:MOST * BLK], right * shrink, 0.0)
        g_send[j] = (gram(1 - side, j) - dot(left, right, 0, 0, EXACT)).astype(BF16)
        g_copy(j).start()
        return carry

    lax.fori_loop(0, hb, send_gram, 0)
    s_part = peer_copy(s_send, sc_recv, 3)
    s_part.start()

    lax.fori_loop(1, n, wait_second, 0)
    project(side, s_own, z_own)

    def keep_gram(j, carry):
        g_own[j] = gram(side, j)
        return carry

    lax.fori_loop(0, hb, keep_gram, 0)
    z_copy.wait()

    def wait_gram(j, carry):
        g_copy(j).wait()
        return carry

    z = z_own[0:PAD_COV, :] + z_recv[0:PAD_COV, :]
    shift = jnp.where(sum_row, z_recv[PAD_COV:32, :] * shrink, 0.0)
    z_minus = jnp.concatenate([-z, shift], axis=0)
    z_plus = jnp.concatenate([z, shift], axis=0)
    for j in range(hb):
        g_own[j] += dot(
            z_minus[:, j * BLK:(j + 1) * BLK], z_plus[:, j * BLK:(j + MOST) * BLK], 0, 0, EXACT
        )
    lax.fori_loop(0, hb, wait_gram, 0)
    s_part.wait()
    scores = s_own[...] + sc_recv[...] - dot(cross, z[:, 0:half], 0, 0, EXACT)

    weight = w_ref[...]
    weight_t = jnp.transpose(
        jnp.concatenate([weight, jnp.zeros((BLK - weight.shape[0], BLK), F32)], axis=0)
    )
    r8 = lax.broadcasted_iota(jnp.int32, (8, BLK), 0)
    l8 = lax.broadcasted_iota(jnp.int32, (8, BLK), 1)
    spread = jnp.concatenate(
        [jnp.where(r8 == j, weight[0:8], 0.0) for j in range(hb)], axis=1
    )
    stat_loc[:, 0:traits] = dot(spread, scores, 1, 1, EXACT)
    stat_loc[:, traits:2 * traits] = dot(spread * spread, scores * scores, 1, 1, EXACT)
    eye = jnp.where(
        lax.broadcasted_iota(jnp.int32, (BLK, BLK), 0)
        == lax.broadcasted_iota(jnp.int32, (BLK, BLK), 1), 1.0, 0.0,
    ).astype(F32)
    lin_rows, sq_rows, diag_rows = [], [], []
    for j in range(hb):
        g = g_own[j] + g_recv[j].astype(F32)
        w_col = weight_t[:, j:j + 1]
        lin_rows.append(jnp.sum(g * w_col, axis=0, keepdims=True))
        sq_rows.append(jnp.sum(g * g * (w_col * w_col), axis=0, keepdims=True))
        diag_rows.append(jnp.sum(g[:, 0:BLK] * eye, axis=0, keepdims=True))
    if hb < 8:
        zero = jnp.zeros((8 - hb, MOST * BLK), F32)
        lin_rows.append(zero)
        sq_rows.append(zero)
        diag_rows.append(zero[:, 0:BLK])
    lin_all = jnp.concatenate(lin_rows, axis=0)
    sq_all = jnp.concatenate(sq_rows, axis=0)
    diag_all = jnp.concatenate(diag_rows, axis=0)
    packed = jnp.zeros((8, BLK), F32)
    for k in range(MOST):
        w_k = weight[k:k + 8]
        twice = 1.0 if k == 0 else 2.0
        first = jnp.sum(lin_all[:, k * BLK:(k + 1) * BLK] * w_k, axis=1, keepdims=True)
        second = jnp.sum(sq_all[:, k * BLK:(k + 1) * BLK] * (w_k * w_k), axis=1, keepdims=True)
        packed = jnp.where(l8 == 2 * k, twice * first, packed)
        packed = jnp.where(l8 == 2 * k + 1, twice * second, packed)
    mean_part = jnp.sum(diag_all * weight[0:8] * weight[0:8], axis=1, keepdims=True)
    packed = jnp.where(l8 == 2 * MOST, mean_part, packed)
    stat_loc[:, 2 * traits:] = packed

    def s_copy(q):
        p = lax.rem(lin + q, 2 * n)
        return pltpu.make_async_remote_copy(
            src_ref=stat_loc,
            dst_ref=stat_all.at[pl.ds(pl.multiple_of(lin * 8, 8), 8)],
            send_sem=t_send.at[q], recv_sem=t_recv.at[q],
            device_id=place(p // 2, lax.rem(p, 2)),
            device_id_type=pl.DeviceIdType.MESH,
        )

    def start_s(q, carry):
        s_copy(q).start()
        return carry

    def wait_s(q, carry):
        s_copy(q).wait()
        return carry

    lax.fori_loop(1, 2 * n, start_s, 0)
    stat_all[pl.ds(pl.multiple_of(lin * 8, 8), 8), :] = stat_loc[...]
    lax.fori_loop(1, 2 * n, wait_s, 0)

    slots = 2 * n * 8
    slot = lax.broadcasted_iota(jnp.int32, (genes, slots), 1)
    within = lax.rem(slot, 8)
    first_variant = ((slot // 8) * hb + within) * BLK
    begin = bounds_ref[:, 0:1]
    end = bounds_ref[:, 1:2]
    inside_gene = (within < hb) & (first_variant >= begin) & (first_variant < end)
    sums = dot(jnp.where(inside_gene, 1.0, 0.0).astype(F32), stat_all[...], 1, 0, EXACT)
    burden_var = sums[:, 2 * traits:2 * traits + 1]
    null_var = sums[:, 2 * traits + 1:2 * traits + 2]
    null_mean = sums[:, 2 * traits + 2 * MOST:2 * traits + 2 * MOST + 1]
    for k in range(1, MOST):
        inside = inside_gene & (first_variant + k * BLK < end)
        pair = dot(
            jnp.where(inside, 1.0, 0.0).astype(F32), stat_all[:, 2 * traits:], 1, 0, EXACT
        )
        burden_var = burden_var + pair[:, 2 * k:2 * k + 1]
        null_var = null_var + pair[:, 2 * k + 1:2 * k + 2]
    null_var = 2.0 * null_var
    burden_ref[...] = sums[:, 0:traits] / jnp.sqrt(burden_var * sigma_sq + 1e-06)
    skat_ref[...] = (sums[:, traits:2 * traits] / sigma_sq - null_mean) / jnp.sqrt(null_var + 1e-06)


def body(genotypes, covariates, phenotypes, variant_weight, gene_start):
    rows, variants = genotypes.shape
    cov = covariates.shape[0]
    traits = phenotypes.shape[0]
    genes = gene_start.shape[0]
    n = lax.axis_size("wide")
    nb = variants // BLK // n
    hb = nb // 2
    span = (nb + HALO) * BLK
    half_span = (hb + HALO) * BLK
    wide = lax.axis_index("wide")
    lin = (lax.rem(wide, n // 2) * 2 + lax.axis_index("sect")) * 2 + wide // (n // 2)
    padded = jnp.concatenate(
        [variant_weight.reshape(-1, BLK), jnp.zeros((16, BLK), F32)], axis=0
    )
    weight = lax.dynamic_slice(padded, (lin * hb, 0), (16, BLK))
    ends = jnp.concatenate([gene_start[1:], jnp.full((1,), variants, jnp.int32)])
    bounds = jnp.stack([gene_start, ends], axis=1)
    vmem = pl.BlockSpec(memory_space=pltpu.VMEM)
    samples = n * rows
    dma = pltpu.SemaphoreType.DMA
    return pl.pallas_call(
        functools.partial(kernel, n, cov, traits, genes, nb),
        out_shape=(
            jax.ShapeDtypeStruct((genes, traits), F32),
            jax.ShapeDtypeStruct((genes, traits), F32),
        ),
        in_specs=[pl.BlockSpec(memory_space=pl.ANY), vmem, vmem, vmem, vmem],
        out_specs=(vmem, vmem),
        scratch_shapes=[
            pltpu.VMEM((rows, variants), jnp.int32),
            pltpu.VMEM((rows, variants + HALO * BLK), BF16),
            pltpu.VMEM((n, rows, span), BF16),
            pltpu.VMEM((PAD_COV + traits, rows), F32),
            pltpu.VMEM((BLK, samples), F32),
            pltpu.VMEM((PAD_COV, BLK), F32),
            pltpu.VMEM((PAD_COV, BLK), F32),
            pltpu.VMEM((PAD_COV + 8, traits), F32),
            pltpu.VMEM((PAD_COV + 8, traits), F32),
            pltpu.VMEM((traits + 96, samples), BF16),
            pltpu.VMEM((hb, BLK, MOST * BLK), BF16),
            pltpu.VMEM((hb, BLK, MOST * BLK), F32),
            pltpu.VMEM((hb, BLK, MOST * BLK), BF16),
            pltpu.VMEM((traits, hb * BLK), F32),
            pltpu.VMEM((traits, hb * BLK), F32),
            pltpu.VMEM((traits, hb * BLK), F32),
            pltpu.VMEM((32, half_span), F32),
            pltpu.VMEM((32, half_span), F32),
            pltpu.VMEM((32, half_span), F32),
            pltpu.VMEM((8, STAT), F32),
            pltpu.VMEM((2 * n * 8, STAT), F32),
            dma((n,)), dma, dma((2, n)), dma((2, n)), dma((n,)), dma((n,)),
            dma((4,)), dma((4,)), dma((2 * n,)), dma((2 * n,)), dma((hb,)), dma((hb,)),
        ],
        compiler_params=pltpu.CompilerParams(
            collective_id=0, has_side_effects=True, vmem_limit_bytes=56 * 1024 * 1024
        ),
        cost_estimate=pl.CostEstimate(
            flops=4 * samples * nb * BLK * MOST * BLK,
            bytes_accessed=rows * variants * 4, transcendentals=0,
        ),
    )(genotypes, covariates, phenotypes, weight, bounds)


def solution(mesh):
    placed = (
        P(("wide", "sect"), "stretch"),
        P(None, ("wide", "sect")),
        P(None, ("wide", "sect")),
        P("stretch"),
        P("stretch"),
    )
    return jax.shard_map(
        body,
        mesh=mesh,
        in_specs=placed,
        out_specs=(P("stretch", None), P("stretch", None)),
        check_vma=False,
    )
```

```python
import functools

import jax
import jax.numpy as jnp
from jax import lax
from jax.experimental import pallas as pl
from jax.experimental.pallas import tpu as pltpu
from jax.sharding import PartitionSpec as P

BLK = 128
MOST = 4
HALO = MOST - 1
PAD_COV = 24
STAT = 256
F32 = jnp.float32
BF16 = jnp.bfloat16
EXACT = lax.Precision.HIGHEST


def dot(a, b, ca, cb, precision=None):
    return lax.dot_general(
        a, b, (((ca,), (cb,)), ((), ())), precision=precision, preferred_element_type=F32
    )


def slots_of(hb):
    groups = []
    for j in range(hb):
        groups.append([(j, 1)] + ([(j + 1, 3)] if j + 1 < hb else []))
    for j in range(hb):
        if j % 4 < 2:
            groups.append([(j, 2)] + ([(j + 2, 2)] if j + 2 < hb else []))
    groups.append([(0, 3)])
    return groups


def kernel(
    n, cov, traits, genes, nb,
    geno, cov_ref, phe_ref, w_ref, start_ref,
    burden_ref, skat_ref,
    stage, sendbuf, recv, xloc, xall, cx_send, cx_all, w_all, m_send, m_recv,
    lhs, g_send, g_own, g_recv, s_send, s_own, sc_recv, z_send, z_own, z_recv, stat_loc, stat_all,
    stage_sem, own_sem, d_send, d_recv, x_send, x_recv, e_send, e_recv, t_send, t_recv, gs_sem, gr_sem, c_send, c_recv,
):
    wide = lax.axis_index("wide")
    member = n // 2
    side = wide // member
    me = lax.rem(wide, member) * 2 + lax.axis_index("sect")
    lin = me * 2 + side

    def place(group, at_side):
        return {"wide": at_side * member + group // 2, "sect": lax.rem(group, 2)}

    rows = geno.shape[0]
    hb = nb // 2
    width = nb * BLK
    span = (nb + HALO) * BLK
    half = hb * BLK
    half_span = (hb + HALO) * BLK
    dof = rows * n * 2 - cov
    peer = {"wide": (1 - side) * member + lax.rem(wide, member)}

    def chunk_copy(c):
        cols = pl.ds(pl.multiple_of(c * width, BLK), width)
        return pltpu.make_async_copy(geno.at[:, cols], stage.at[:, cols], stage_sem.at[c])

    def start_chunk(t, carry):
        chunk_copy(lax.rem(me - t + n, n)).start()
        return carry

    lax.fori_loop(0, n, start_chunk, 0)

    xloc[...] = jnp.zeros_like(xloc)
    xloc[0:cov, :] = cov_ref[...]
    xloc[PAD_COV:PAD_COV + traits, :] = phe_ref[...]
    xall[...] = jnp.zeros_like(xall)
    blocks = w_ref.shape[0]
    w_all[0:blocks, :] = w_ref[...]
    w_all[blocks:, :] = jnp.zeros((16, BLK), F32)
    sendbuf[:, n * width:] = jnp.zeros((rows, HALO * BLK), BF16)

    barrier = pltpu.get_barrier_semaphore()

    def greet(q, carry):
        p = lax.rem(lin + q, 2 * n)
        pl.semaphore_signal(
            barrier, inc=1, device_id=place(p // 2, lax.rem(p, 2)),
            device_id_type=pl.DeviceIdType.MESH,
        )
        return carry

    lax.fori_loop(1, 2 * n, greet, 0)
    pl.semaphore_wait(barrier, 2 * n - 1)

    xrows = PAD_COV + traits

    def x_copy(t):
        return pltpu.make_async_remote_copy(
            src_ref=xloc.at[0:xrows],
            dst_ref=xall.at[0:xrows, pl.ds(pl.multiple_of(me * rows, BLK), rows)],
            send_sem=x_send.at[t], recv_sem=x_recv.at[t],
            device_id=place(lax.rem(me - t + n, n), side),
            device_id_type=pl.DeviceIdType.MESH,
        )

    def d_part(t, part, offset, size):
        c = lax.rem(me - t + n, n)
        return pltpu.make_async_remote_copy(
            src_ref=sendbuf.at[:, pl.ds(pl.multiple_of(c * width + offset, BLK), size)],
            dst_ref=recv.at[me, :, pl.ds(pl.multiple_of(offset, BLK), size)],
            send_sem=d_send.at[part, t], recv_sem=d_recv.at[part, t],
            device_id=place(c, side),
            device_id_type=pl.DeviceIdType.MESH,
        )

    def d_first(t):
        return d_part(t, 0, (1 - side) * half, half_span)

    def d_second(t):
        return d_part(t, 1, side * half_span, half)

    def start_x(t, carry):
        x_copy(t).start()
        return carry

    lax.fori_loop(1, n, start_x, 0)
    xall[0:xrows, pl.ds(pl.multiple_of(me * rows, BLK), rows)] = xloc[0:xrows, :]

    def c_copy(q):
        p = lax.rem(lin + q, 2 * n)
        return pltpu.make_async_remote_copy(
            src_ref=cx_send, dst_ref=cx_all.at[lin],
            send_sem=c_send.at[q], recv_sem=c_recv.at[q],
            device_id=place(p // 2, lax.rem(p, 2)),
            device_id_type=pl.DeviceIdType.MESH,
        )

    def start_c(q, carry):
        c_copy(q).start()
        return carry

    def wait_c(q, carry):
        c_copy(q).wait()
        return carry

    cx_send[...] = dot(xloc[0:PAD_COV, :], xloc[...], 1, 1, EXACT)
    lax.fori_loop(1, 2 * n, start_c, 0)
    cx_all[lin] = cx_send[...]

    def convert(c):
        chunk_copy(c).wait()
        cols = pl.ds(pl.multiple_of(c * width, BLK), width)
        sendbuf[:, cols] = stage[:, cols].astype(F32).astype(BF16)

    convert(me)

    def send_chunk(t, carry):
        convert(lax.rem(me - t + n, n))
        d_first(t).start()
        return carry

    def send_second(t, carry):
        d_second(t).start()
        return carry

    lax.fori_loop(1, n, send_chunk, 0)
    own_copy = pltpu.make_async_copy(
        sendbuf.at[:, pl.ds(pl.multiple_of(me * width, BLK), span)], recv.at[me], own_sem
    )
    own_copy.start()

    def wait_x(t, carry):
        x_copy(t).wait()
        return carry

    lax.fori_loop(1, n, wait_x, 0)

    def peer_copy(src, dst, k):
        return pltpu.make_async_remote_copy(
            src_ref=src, dst_ref=dst, send_sem=e_send.at[k], recv_sem=e_recv.at[k],
            device_id=peer, device_id_type=pl.DeviceIdType.MESH,
        )

    call = xall[0:PAD_COV, :]
    lax.fori_loop(1, 2 * n, wait_c, 0)
    row = lax.broadcasted_iota(jnp.int32, (PAD_COV, BLK), 0)
    lane = lax.broadcasted_iota(jnp.int32, (PAD_COV, BLK), 1)
    mat = jnp.sum(cx_all[...], axis=0) + jnp.where(lane == row + 96, 1.0, 0.0).astype(F32)
    for j in range(cov):
        scale = 1.0 / jnp.sqrt(mat[j:j + 1, j:j + 1])
        row_j = mat[j:j + 1, :] * scale
        col_j = mat[:, j:j + 1] * scale
        mat = jnp.where(row > j, mat - col_j * row_j, jnp.where(row == j, row_j, mat))
    proj = mat[:, PAD_COV:PAD_COV + traits]
    low_inv = mat[:, 96:96 + PAD_COV]
    cov_unit = dot(low_inv, call, 1, 0, EXACT)
    resid = xall[PAD_COV:PAD_COV + traits, :] - dot(proj, cov_unit, 0, 0, EXACT)
    resid_low = resid.astype(BF16)
    lhs[...] = jnp.zeros_like(lhs)
    lhs[0:traits, :] = resid_low
    hi = cov_unit.astype(BF16)
    rest = cov_unit - hi.astype(F32)
    mid = rest.astype(BF16)
    low = (rest - mid.astype(F32)).astype(BF16)
    lhs[traits:traits + PAD_COV, :] = hi
    lhs[traits + 32:traits + 32 + PAD_COV, :] = mid
    lhs[traits + 24:traits + 32, :] = jnp.ones((8, lhs.shape[1]), BF16)
    lhs[traits + 64:traits + 64 + PAD_COV, :] = low
    m_send[0:PAD_COV, :] = dot(cov_unit, resid_low.astype(F32), 1, 1, EXACT)
    ones = jnp.ones((8, resid.shape[1]), F32)
    m_send[PAD_COV:PAD_COV + 8, :] = dot(ones, resid * resid, 1, 1, EXACT)
    m_copy = peer_copy(m_send, m_recv, 0)
    m_copy.start()
    own_copy.wait()

    def wait_first(t, carry):
        d_first(t).wait()
        return carry

    def wait_second(t, carry):
        d_second(t).wait()
        return carry

    def gram(which, j):
        at = pl.multiple_of(which * half + j * BLK, BLK)
        left = recv[:, :, pl.ds(at, BLK)].reshape(n * rows, BLK)
        right = recv[:, :, pl.ds(at, MOST * BLK)].reshape(n * rows, MOST * BLK)
        return dot(left, right, 0, 0)

    def project(which, s_out, z_out):
        base = pl.multiple_of(which * half, BLK)
        data = recv[:, :, pl.ds(base, half_span)].reshape(n * rows, half_span)
        full = dot(lhs[...], data, 1, 0)
        s_out[...] = full[0:traits, 0:half]
        z_out[...] = (
            full[traits:traits + 32] + full[traits + 32:traits + 64] + full[traits + 64:traits + 96]
        )

    shrink = 1.0 / float(n * rows) ** 0.5

    def diag_copy(j):
        return pltpu.make_async_remote_copy(
            src_ref=g_send.at[j], dst_ref=g_recv.at[j],
            send_sem=gs_sem.at[j], recv_sem=gr_sem.at[j],
            device_id=peer, device_id_type=pl.DeviceIdType.MESH,
        )

    lax.fori_loop(1, n, wait_first, 0)
    project(1 - side, s_send, z_send)
    z_copy = peer_copy(z_send, z_recv, 1)
    z_copy.start()
    sum_row = lax.broadcasted_iota(jnp.int32, (8, half_span), 0) == 0

    def send_gram(j, carry):
        left = z_send[PAD_COV:32, pl.ds(pl.multiple_of(j * BLK, BLK), BLK)]
        right = z_send[PAD_COV:32, pl.ds(pl.multiple_of(j * BLK, BLK), MOST * BLK)]
        left = jnp.where(sum_row[:, 0:BLK], left * shrink, 0.0)
        right = jnp.where(sum_row[:, 0:MOST * BLK], right * shrink, 0.0)
        centred = gram(1 - side, j) - dot(left, right, 0, 0, EXACT)
        g_send[j] = centred[:, 0:BLK].astype(BF16)
        diag_copy(j).start()
        g_own[j] = centred
        return carry

    lax.fori_loop(0, hb, send_gram, 0)
    start_row = jnp.broadcast_to(start_ref[...], (genes, genes)).astype(F32)
    gene_r = lax.broadcasted_iota(jnp.int32, (genes, genes), 0)
    gene_c = lax.broadcasted_iota(jnp.int32, (genes, genes), 1)
    begin = jnp.sum(jnp.where(gene_c == gene_r, start_row, 0.0), axis=1, keepdims=True)
    end = jnp.sum(jnp.where(gene_c == gene_r + 1, start_row, 0.0), axis=1, keepdims=True)
    end = jnp.where(gene_r[:, 0:1] == genes - 1, float(n * width), end)
    begin = begin.astype(jnp.int32)
    end = end.astype(jnp.int32)
    peer_first = (
        me * nb + (1 - side) * hb + lax.broadcasted_iota(jnp.int32, (genes, BLK), 1)
    ) * BLK
    same = [None]
    for k in range(1, MOST):
        both = (peer_first >= begin) & (peer_first + k * BLK < end)
        same.append(jnp.sum(jnp.where(both, 1.0, 0.0).astype(F32), axis=0, keepdims=True))
    for index, pairs in enumerate(slots_of(hb)):
        total = None
        for j, k in pairs:
            term = g_own[j, :, k * BLK:(k + 1) * BLK] * same[k][:, j:j + 1]
            total = term if total is None else total + term
        g_send[hb + index] = total.astype(BF16)
    g_rest = peer_copy(g_send.at[hb:], g_recv.at[hb:], 3)
    g_rest.start()
    s_part = peer_copy(s_send, sc_recv, 2)
    s_part.start()
    lax.fori_loop(1, n, send_second, 0)

    lax.fori_loop(1, n, wait_second, 0)
    project(side, s_own, z_own)

    def keep_gram(j, carry):
        g_own[j] = gram(side, j)
        return carry

    lax.fori_loop(0, hb, keep_gram, 0)
    z_copy.wait()

    def wait_gram(j, carry):
        diag_copy(j).wait()
        return carry

    z = z_own[0:PAD_COV, :] + z_recv[0:PAD_COV, :]
    shift = jnp.where(sum_row, z_recv[PAD_COV:32, :] * shrink, 0.0)
    z_minus = jnp.concatenate([-z, shift], axis=0)
    z_plus = jnp.concatenate([z, shift], axis=0)
    for j in range(hb):
        g_own[j] += dot(
            z_minus[:, j * BLK:(j + 1) * BLK], z_plus[:, j * BLK:(j + MOST) * BLK], 0, 0, EXACT
        )
    lax.fori_loop(0, hb, wait_gram, 0)
    g_rest.wait()
    where_is = {pair: hb + i for i, pairs in enumerate(slots_of(hb)) for pair in pairs}
    s_part.wait()
    m_copy.wait()
    cross = m_send[0:PAD_COV, :] + m_recv[0:PAD_COV, :]
    sigma_sq = (m_send[PAD_COV:PAD_COV + 1, :] + m_recv[PAD_COV:PAD_COV + 1, :]) / dof
    scores = s_own[...] + sc_recv[...] - dot(cross, z[:, 0:half], 0, 0, EXACT)

    weight = w_all[pl.ds(lin * hb, 16), :]
    weight_t = jnp.transpose(
        jnp.concatenate([weight, jnp.zeros((BLK - weight.shape[0], BLK), F32)], axis=0)
    )
    r8 = lax.broadcasted_iota(jnp.int32, (8, BLK), 0)
    l8 = lax.broadcasted_iota(jnp.int32, (8, BLK), 1)
    spread = jnp.concatenate(
        [jnp.where(r8 == j, weight[0:8], 0.0) for j in range(hb)], axis=1
    )
    stat_loc[:, 0:traits] = dot(spread, scores, 1, 1, EXACT)
    stat_loc[:, traits:2 * traits] = dot(spread * spread, scores * scores, 1, 1, EXACT)
    eye = jnp.where(
        lax.broadcasted_iota(jnp.int32, (BLK, BLK), 0)
        == lax.broadcasted_iota(jnp.int32, (BLK, BLK), 1), 1.0, 0.0,
    ).astype(F32)
    lin_rows, sq_rows, diag_rows = [], [], []
    for j in range(hb):
        g = g_own[j] + jnp.concatenate(
            [g_recv[j]] + [g_recv[where_is[j, k]] for k in range(1, MOST)], axis=1
        ).astype(F32)
        w_col = weight_t[:, j:j + 1]
        lin_rows.append(jnp.sum(g * w_col, axis=0, keepdims=True))
        sq_rows.append(jnp.sum(g * g * (w_col * w_col), axis=0, keepdims=True))
        diag_rows.append(jnp.sum(g[:, 0:BLK] * eye, axis=0, keepdims=True))
    if hb < 8:
        zero = jnp.zeros((8 - hb, MOST * BLK), F32)
        lin_rows.append(zero)
        sq_rows.append(zero)
        diag_rows.append(zero[:, 0:BLK])
    lin_all = jnp.concatenate(lin_rows, axis=0)
    sq_all = jnp.concatenate(sq_rows, axis=0)
    diag_all = jnp.concatenate(diag_rows, axis=0)
    packed = jnp.zeros((8, BLK), F32)
    for k in range(MOST):
        w_k = weight[k:k + 8]
        twice = 1.0 if k == 0 else 2.0
        first = jnp.sum(lin_all[:, k * BLK:(k + 1) * BLK] * w_k, axis=1, keepdims=True)
        second = jnp.sum(sq_all[:, k * BLK:(k + 1) * BLK] * (w_k * w_k), axis=1, keepdims=True)
        packed = jnp.where(l8 == 2 * k, twice * first, packed)
        packed = jnp.where(l8 == 2 * k + 1, twice * second, packed)
    mean_part = jnp.sum(diag_all * weight[0:8] * weight[0:8], axis=1, keepdims=True)
    packed = jnp.where(l8 == 2 * MOST, mean_part, packed)
    stat_loc[:, 2 * traits:] = packed

    def s_copy(q):
        p = lax.rem(lin + q, 2 * n)
        return pltpu.make_async_remote_copy(
            src_ref=stat_loc,
            dst_ref=stat_all.at[pl.ds(pl.multiple_of(lin * 8, 8), 8)],
            send_sem=t_send.at[q], recv_sem=t_recv.at[q],
            device_id=place(p // 2, lax.rem(p, 2)),
            device_id_type=pl.DeviceIdType.MESH,
        )

    def start_s(q, carry):
        s_copy(q).start()
        return carry

    def wait_s(q, carry):
        s_copy(q).wait()
        return carry

    lax.fori_loop(1, 2 * n, start_s, 0)
    stat_all[pl.ds(pl.multiple_of(lin * 8, 8), 8), :] = stat_loc[...]
    lax.fori_loop(1, 2 * n, wait_s, 0)

    slots = 2 * n * 8
    slot = lax.broadcasted_iota(jnp.int32, (genes, slots), 1)
    within = lax.rem(slot, 8)
    first_variant = ((slot // 8) * hb + within) * BLK
    inside_gene = (within < hb) & (first_variant >= begin) & (first_variant < end)
    sums = dot(jnp.where(inside_gene, 1.0, 0.0).astype(F32), stat_all[...], 1, 0, EXACT)
    burden_var = sums[:, 2 * traits:2 * traits + 1]
    null_var = sums[:, 2 * traits + 1:2 * traits + 2]
    null_mean = sums[:, 2 * traits + 2 * MOST:2 * traits + 2 * MOST + 1]
    for k in range(1, MOST):
        inside = inside_gene & (first_variant + k * BLK < end)
        pair = dot(
            jnp.where(inside, 1.0, 0.0).astype(F32), stat_all[:, 2 * traits:], 1, 0, EXACT
        )
        burden_var = burden_var + pair[:, 2 * k:2 * k + 1]
        null_var = null_var + pair[:, 2 * k + 1:2 * k + 2]
    null_var = 2.0 * null_var
    burden_ref[...] = sums[:, 0:traits] / jnp.sqrt(burden_var * sigma_sq + 1e-06)
    skat_ref[...] = (sums[:, traits:2 * traits] / sigma_sq - null_mean) / jnp.sqrt(null_var + 1e-06)


def body(genotypes, covariates, phenotypes, variant_weight, gene_start):
    rows, variants = genotypes.shape
    cov = covariates.shape[0]
    traits = phenotypes.shape[0]
    genes = gene_start.shape[0]
    n = lax.axis_size("wide")
    nb = variants // BLK // n
    hb = nb // 2
    span = (nb + HALO) * BLK
    half_span = (hb + HALO) * BLK
    vmem = pl.BlockSpec(memory_space=pltpu.VMEM)
    samples = n * rows
    dma = pltpu.SemaphoreType.DMA
    return pl.pallas_call(
        functools.partial(kernel, n, cov, traits, genes, nb),
        out_shape=(
            jax.ShapeDtypeStruct((genes, traits), F32),
            jax.ShapeDtypeStruct((genes, traits), F32),
        ),
        in_specs=[pl.BlockSpec(memory_space=pl.ANY), vmem, vmem, vmem, vmem],
        out_specs=(vmem, vmem),
        scratch_shapes=[
            pltpu.VMEM((rows, variants), jnp.int32),
            pltpu.VMEM((rows, variants + HALO * BLK), BF16),
            pltpu.VMEM((n, rows, span), BF16),
            pltpu.VMEM((BLK, rows), F32),
            pltpu.VMEM((BLK, samples), F32),
            pltpu.VMEM((PAD_COV, BLK), F32),
            pltpu.VMEM((2 * n, PAD_COV, BLK), F32),
            pltpu.VMEM((variants // BLK + 16, BLK), F32),
            pltpu.VMEM((PAD_COV + 8, traits), F32),
            pltpu.VMEM((PAD_COV + 8, traits), F32),
            pltpu.VMEM((traits + 96, samples), BF16),
            pltpu.VMEM((hb + len(slots_of(hb)), BLK, BLK), BF16),
            pltpu.VMEM((hb, BLK, MOST * BLK), F32),
            pltpu.VMEM((hb + len(slots_of(hb)), BLK, BLK), BF16),
            pltpu.VMEM((traits, hb * BLK), F32),
            pltpu.VMEM((traits, hb * BLK), F32),
            pltpu.VMEM((traits, hb * BLK), F32),
            pltpu.VMEM((32, half_span), F32),
            pltpu.VMEM((32, half_span), F32),
            pltpu.VMEM((32, half_span), F32),
            pltpu.VMEM((8, STAT), F32),
            pltpu.VMEM((2 * n * 8, STAT), F32),
            dma((n,)), dma, dma((2, n)), dma((2, n)), dma((n,)), dma((n,)),
            dma((4,)), dma((4,)), dma((2 * n,)), dma((2 * n,)), dma((hb,)), dma((hb,)),
            dma((2 * n,)), dma((2 * n,)),
        ],
        compiler_params=pltpu.CompilerParams(
            collective_id=0, has_side_effects=True, vmem_limit_bytes=56 * 1024 * 1024
        ),
        cost_estimate=pl.CostEstimate(
            flops=4 * samples * nb * BLK * MOST * BLK,
            bytes_accessed=rows * variants * 4, transcendentals=0,
        ),
    )(genotypes, covariates, phenotypes, variant_weight.reshape(-1, BLK), gene_start.reshape(1, genes))


def solution(mesh):
    placed = (
        P(("wide", "sect"), "stretch"),
        P(None, ("wide", "sect")),
        P(None, ("wide", "sect")),
        P("stretch"),
        P("stretch"),
    )
    return jax.shard_map(
        body,
        mesh=mesh,
        in_specs=placed,
        out_specs=(P("stretch", None), P("stretch", None)),
        check_vma=False,
    )
```
